32 devices in a mesh: groups: 2 (over y), store: 4 (over z), head: 2 (over x), sub: 2 (over core).
Axes of the slice: x: 2, y: 2, z: 4, core: 2. Of those that a mesh axis runs over, the one named last changes fastest.
Arguments:
- fresh_query: bfloat16 [16, 528, 8192], P(('groups', 'store'), None, ('head', 'sub')), parts along dimension 0, may hold values from -20 to 20
- fresh_keys: bfloat16 [16, 528, 1024], P(('groups', 'store'), None, 'head'), parts along dimension 0, may hold values from -6 to 6
- fresh_values: bfloat16 [16, 528, 1024], P(('groups', 'store'), None, 'head'), parts along dimension 0, may hold values from -24 to 24
- store_keys: bfloat16 [64, 512, 1024], P(('groups', 'store'), 'sub', 'head'), parts along dimension 0, may hold values from -6 to 6
- store_values: bfloat16 [64, 512, 1024], P(('groups', 'store'), 'sub', 'head'), parts along dimension 0, may hold values from -24 to 24
- span_ids: int32 [16, 6], P('groups'), parts along dimension 0, may hold values from 0 to 31, as said below
- span_slot: int32 [64], P('groups'), parts along dimension 0, may hold values from 0 to 31, as said below
- select_pos: int32 [16, 464], P('groups'), parts along dimension 0, may hold values from 0 to 3071, as said below
- ask_len: int32 [16], P('groups'), parts along dimension 0, may hold values from 1 to 64, as said below
Outputs:
- attn_out: bfloat16 [16, 528, 8192], P(('groups', 'store'), None, ('head', 'sub')), parts along dimension 0
The draws below stay inside these ranges and needn't reach their ends.
There are 2 independent parts, one for each index of `groups`. The reference program is written for one: setup_inputs(seed, part) draws one part's arguments, and reference() takes and returns one part's arrays. A program takes and returns all parts, laid end to end along the dimension named above; each array names one. Nothing has to cross between parts.
Inputs may be any that keep to these rules, and one draw needn't show every extreme that they name: `span_ids`: the 6 spans of a request are distinct. Over the 2 requests of one store index (requests s * 2 to s * 2 + 1) all named spans are distinct, and at most 3 of them have slots on any one store index, exactly 3 on some. `span_slot`: A permutation; the span with slot v is held by store index v // 8. `select_pos`: strictly increasing within each request. `ask_len`: some request has 64.
All inputs are finite; a program needn't handle non-finite values.
Results may differ from the reference program's by a relative error of at most 0.0045.
Values may be sent and summed in bfloat16 or wider, within the bound.
A program may use at most 128 MiB of HBM per device.

```python
import jax
import jax.numpy as jnp
from jax import lax

HD = 128
QH = 64
KVH = 8
GROUP = 8
SPAN = 512
NCH = 6
CTX = 3072
SEL = 464
QLEN = 64
ROWS = 528
REQ_DEV = 2
CH_DEV = 8
REQS = 8
NCHUNKS = 32
N_STORE = 4


def span_layout(key):
    key_perm, key_owner, key_base = jax.random.split(jax.random.fold_in(key, 7), 3)
    slot_of = jax.random.permutation(key_perm, NCHUNKS).astype(jnp.int32)
    span_at = jnp.argsort(slot_of).astype(jnp.int32)
    references = REQ_DEV * NCH
    owner_scores = jax.random.randint(key_owner, (N_STORE, N_STORE), 0, 1 << 20) * N_STORE + jnp.arange(N_STORE)[None, :]
    owner_order = jnp.argsort(owner_scores, axis=1).astype(jnp.int32)
    base_picks = jax.random.randint(key_base, (3, N_STORE, N_STORE), 0, CH_DEV)
    base_place = jnp.min(base_picks, axis=0)
    counter = jnp.arange(references)
    owners = owner_order[:, counter % N_STORE]
    turns = counter // N_STORE
    starts = jnp.take_along_axis(base_place, owners, axis=1)
    slot_ids = owners * CH_DEV + (starts + turns[None, :]) % CH_DEV
    span_names = span_at[slot_ids].reshape(N_STORE * REQ_DEV, NCH)
    return (span_names.astype(jnp.int32), slot_of)


def draw_span_ids(key, part):
    return span_layout(key)[0]


def draw_span_slot(key, part):
    return span_layout(key)[1]


def draw_select_pos(key, part):
    scores = jax.random.randint(jax.random.fold_in(key, 11), (REQS, CTX), 0, 1 << 18) * CTX + jnp.arange(CTX)[None, :]
    picked = jnp.argsort(scores, axis=1)[:, :SEL]
    return jnp.sort(picked, axis=1).astype(jnp.int32)


def draw_ask_len(key, part):
    key_len, key_spot = jax.random.split(jax.random.fold_in(key, 13))
    lengths = jax.random.randint(key_len, (REQS,), 1, QLEN + 1)
    spot = jax.random.randint(key_spot, (), 0, REQS)
    return jnp.where(jnp.arange(REQS) == spot, QLEN, lengths).astype(jnp.int32)


def drawn_rows(key):
    parts_keys = jax.random.split(jax.random.fold_in(key, 17), 2)
    row_keys = jax.random.truncated_normal(parts_keys[0], -6.0, 6.0, (REQS, ROWS, KVH * HD), jnp.float32)
    row_query = jax.random.truncated_normal(parts_keys[1], -6.0, 6.0, (REQS, ROWS, QH * HD), jnp.float32)
    return (row_keys, row_query)


def draw_fresh_keys(key, part):
    return drawn_rows(key)[0].astype(jnp.bfloat16)


def draw_fresh_query(key, part):
    return drawn_rows(key)[1].astype(jnp.bfloat16)


def levels(key, dims, cuts, low, largest):
    def one(axis_at, shards_of):
        draws = jax.random.uniform(jax.random.fold_in(jax.random.fold_in(key, 6), axis_at), (shards_of,), jnp.float32, low / len(cuts), largest / len(cuts))
        return jnp.repeat(jnp.exp(draws), dims[axis_at] // shards_of).reshape((-1,) + (1,) * (len(dims) - axis_at - 1))

    loudness = one(*cuts[0])
    for cut in cuts[1:]:
        loudness = loudness * one(*cut)
    return loudness


def scatter_about(key, dims, deviation, reach, shards=(), kind=jnp.bfloat16):
    result = jax.random.normal(key, dims, jnp.float32) * deviation
    if len(shards) > 0:
        result = levels(key, dims, shards, -0.22, 0.18) * result
    return jnp.clip(result, min=-reach, max=reach).astype(kind)


def setup_inputs(seed: int = 0, part: int = 0) -> dict:
    keys = jax.random.split(jax.random.key(seed), 10)
    own_keys = jax.random.split(jax.random.fold_in(keys[9], part), 10)
    return {
        "fresh_query": draw_fresh_query(jax.random.fold_in(jax.random.fold_in(keys[9], part), 71), part),
        "fresh_keys": draw_fresh_keys(jax.random.fold_in(jax.random.fold_in(keys[9], part), 71), part),
        "fresh_values": scatter_about(own_keys[2], (REQS, ROWS, KVH * HD), 4.0, 24.0, ((0, 4), (2, 2))),
        "store_keys": scatter_about(own_keys[3], (NCHUNKS, SPAN, KVH * HD), 1.0, 6.0, ((0, 4), (1, 2), (2, 2))),
        "store_values": scatter_about(own_keys[4], (NCHUNKS, SPAN, KVH * HD), 4.0, 24.0, ((0, 4), (1, 2), (2, 2))),
        "span_ids": draw_span_ids(jax.random.fold_in(jax.random.fold_in(keys[9], part), 71), part),
        "span_slot": draw_span_slot(jax.random.fold_in(jax.random.fold_in(keys[9], part), 71), part),
        "select_pos": draw_select_pos(jax.random.fold_in(jax.random.fold_in(keys[9], part), 71), part),
        "ask_len": draw_ask_len(jax.random.fold_in(jax.random.fold_in(keys[9], part), 71), part),
    }


NEGATIVE = -1.0e30


def reference(fresh_query, fresh_keys, fresh_values, store_keys, store_values, span_ids, span_slot, select_pos, ask_len):
    slot_ids = span_slot[span_ids]
    score_scale = HD ** -0.5

    def per_request(pieces):
        query_rows, key_rows, value_rows, request_slots, positions, ask_length = pieces
        context_keys = store_keys[request_slots].reshape(CTX, KVH * HD)
        context_values = store_values[request_slots].reshape(CTX, KVH * HD)
        context_keys = context_keys.at[positions].set(key_rows[:SEL])
        context_values = context_values.at[positions].set(value_rows[:SEL])
        all_keys = jnp.concatenate([context_keys, key_rows[SEL:]], axis=0)
        all_values = jnp.concatenate([context_values, value_rows[SEL:]], axis=0)
        query_pos = jnp.concatenate([positions, CTX + jnp.arange(QLEN, dtype=jnp.int32)])
        key_pos = jnp.arange(CTX + QLEN, dtype=jnp.int32)
        key_live = key_pos < CTX + ask_length
        allowed = (key_pos[None, :] <= query_pos[:, None]) & key_live[None, :]
        row_live = jnp.arange(ROWS, dtype=jnp.int32) < SEL + ask_length

        def per_head(kv_head):
            head_keys = lax.dynamic_slice_in_dim(all_keys, kv_head * HD, HD, 1).astype(jnp.float32)
            head_values = lax.dynamic_slice_in_dim(all_values, kv_head * HD, HD, 1).astype(jnp.float32)
            head_query = lax.dynamic_slice_in_dim(query_rows, kv_head * GROUP * HD, GROUP * HD, 1)
            head_query = head_query.astype(jnp.float32).reshape(ROWS, GROUP, HD)
            scores = jnp.einsum("rgd,kd->grk", head_query, head_keys) * score_scale
            scores = jnp.where(allowed[None], scores, NEGATIVE)
            row_max = jnp.max(scores, axis=-1, keepdims=True)
            powers = jnp.where(allowed[None], jnp.exp(scores - row_max), 0.0)
            totals = jnp.sum(powers, axis=-1)
            weights = lax.optimization_barrier(powers.astype(jnp.bfloat16)).astype(jnp.float32)
            mixed = jnp.einsum("grk,kd->rgd", weights, head_values)
            return mixed / jnp.transpose(totals)[:, :, None]

        heads_out = lax.map(per_head, jnp.arange(KVH, dtype=jnp.int32))
        merged = jnp.transpose(heads_out, (1, 0, 2, 3)).reshape(ROWS, QH * HD)
        return jnp.where(row_live[:, None], merged, 0.0).astype(jnp.bfloat16)

    return lax.map(per_request, (fresh_query, fresh_keys, fresh_values, slot_ids, select_pos, ask_len))
```

```python
import functools
import math

import jax
import jax.numpy as jnp
from jax import lax
from jax.experimental import pallas as pl
from jax.experimental.pallas import tpu as pltpu
from jax.sharding import PartitionSpec as P

HD = 128
GROUP = 8
NEGATIVE = -1e30
FAR = 1 << 20
CHAIN = 2
VMEM_BYTES = 52 * 1024 * 1024


def row_tile(rows):
    for size in range(192, 15, -16):
        if rows % size == 0:
            return size
    return rows


def round_up(value, unit):
    return (value + unit - 1) // unit * unit


def pack_kernel(stores, capacity, req_dev, nch, ch_dev, q_heads, kv_used, ids, slots, keys, values, *rest):
    outs = rest[: 2 * stores]
    sems = rest[2 * stores]
    me = lax.axis_index("store")
    core = lax.axis_index("sub")
    width = kv_used * HD

    def copies(d, e, place, rank):
        column = pl.multiple_of(lax.rem(core + e, 2) * q_heads // GROUP * HD, HD)
        return [
            pltpu.make_async_copy(
                source.at[place, :, pl.ds(column, width)],
                outs[2 * d + e].at[rank, which],
                sems.at[((d * capacity + rank) * 2 + e) * 2 + which],
            )
            for which, source in enumerate((keys, values))
        ]

    counts = []
    for step in range(stores):
        d = (step + 1) % stores
        target = lax.rem(me + d, stores)

        def visit(j, rank):
            request = target * req_dev + lax.div(j, nch)
            slot = slots[ids[request, lax.rem(j, nch)]]
            place = lax.rem(slot, ch_dev)
            hit = lax.div(slot, ch_dev) == me

            @pl.when(hit)
            def _():
                for e in range(2):
                    for copy in copies(d, e, place, rank):
                        copy.start()

            return rank + hit.astype(jnp.int32)

        counts.append((d, lax.fori_loop(0, req_dev * nch, visit, jnp.int32(0))))
    for d, count in counts:

        def finish(rank, unused):
            for e in range(2):
                for copy in copies(d, e, 0, rank):
                    copy.wait()
            return unused

        lax.fori_loop(0, count, finish, 0)


def attend_kernel(offsets, first, last, per_kv, nch, select, rows, tile, half, *refs):
    table, lens, column, q_ref, kf_ref, vf_ref, qpos_ref, kpos_ref = refs[:8]
    pieces = refs[8 : 8 + 2 * len(offsets)]
    rest = list(refs[8 + 2 * len(offsets) :])
    if not first:
        acc_in, ml_in = rest[:2]
        rest = rest[2:]
    if last:
        out_ref = rest[0]
        rest = rest[1:]
    else:
        acc_out, ml_out = rest[:2]
        rest = rest[2:]
    acc_ref, m_ref, k_scr, v_scr, page_v = rest
    request = pl.program_id(0)
    scale = HD ** (-0.5) * math.log2(math.e)
    chain = min(CHAIN, per_kv)
    tiles = rows // tile
    lens_here = lens[request]

    def wide(value, width):
        return jnp.concatenate([value] * (width // HD), axis=1)

    def attend(spot, row_at, keys, values, biases, begin):
        heads = pl.ds(spot * chain, chain)
        span = pl.ds(row_at, tile)
        q = jnp.concatenate(
            [q_ref[0, span, (spot * chain + h) * HD : (spot * chain + h + 1) * HD] for h in range(chain)], axis=0
        )
        scores = []
        for k, bias in zip(keys, biases):
            s = lax.dot_general(q, k, (((1,), (1,)), ((), ())), preferred_element_type=jnp.float32)
            s = s.reshape(chain, tile, s.shape[1]) + bias[None]
            scores.append(s.reshape(chain * tile, s.shape[2]))
        peak = jnp.max(scores[0], axis=-1, keepdims=True)
        for s in scores[1:]:
            peak = jnp.maximum(peak, jnp.max(s, axis=-1, keepdims=True))
        if begin:
            m_new = jnp.broadcast_to(peak, (chain * tile, HD))
        else:
            m_old = m_ref[heads, span, :].reshape(chain * tile, HD)
            m_new = jnp.maximum(m_old, peak)
        update = None
        for s, v in zip(scores, values):
            p = jnp.exp2((s - wide(m_new, s.shape[1])) * scale).astype(jnp.bfloat16)
            part = jnp.dot(p, v, preferred_element_type=jnp.float32)
            update = part if update is None else update + part
        if not begin:
            factor = jnp.exp2((m_old - m_new) * scale)
            update = acc_ref[heads, span, :].reshape(chain * tile, 2 * HD) * wide(factor, 2 * HD) + update
        acc_ref[heads, span, :] = update.reshape(chain, tile, 2 * HD)
        m_ref[heads, span, :] = m_new.reshape(chain, tile, HD)

    page_v[:, :, HD:] = jnp.ones((2, half, HD), jnp.bfloat16)
    if first:
        padded = k_scr.shape[0]
        k_scr[...] = jnp.zeros(k_scr.shape, jnp.bfloat16)
        v_scr[:, :HD] = jnp.zeros((padded, HD), jnp.bfloat16)
        v_scr[:, HD:] = jnp.ones((padded, HD), jnp.bfloat16)
        k_scr[:rows, :] = kf_ref[0]
        v_scr[:rows, :HD] = vf_ref[0]
        for t in range(tiles):
            end = min(round_up((t + 1) * tile, HD), padded)
            row_id = lax.broadcasted_iota(jnp.int32, (tile, end), 0) + t * tile
            key_id = lax.broadcasted_iota(jnp.int32, (tile, end), 1)
            allowed = (key_id <= row_id) & (key_id < select + lens_here)
            bias = jnp.where(allowed, 0.0, NEGATIVE)
            for spot in range(per_kv // chain):
                attend(spot, t * tile, [k_scr[:end, :]], [v_scr[:end, :]], [bias], True)
    else:
        ml = ml_in[0]
        acc_ref[:, :, :HD] = acc_in[0]
        m_ref[...] = jnp.broadcast_to(ml[:, :, :1], ml.shape)
        acc_ref[:, :, HD:] = jnp.broadcast_to(ml[:, :, HD // 2 : HD // 2 + 1], ml.shape)

    core = lax.axis_index("sub")

    def page(chunk, unused):
        base = (request * nch + chunk) * 3
        offset, rank, tile_from = table[base], table[base + 1], table[base + 2]
        for at, d in enumerate(offsets):

            @pl.when(offset == d)
            def _():
                keys = [pieces[2 * at + e][rank, 0] for e in range(2)]
                for e in range(2):
                    page_v[e, :, :HD] = pieces[2 * at + e][rank, 1]
                kpos = [kpos_ref[0, chunk * 2 + lax.rem(core + e, 2)] for e in range(2)]

                def one_tile(t, unused):
                    row_at = pl.multiple_of(t * tile, 16)
                    qpos = qpos_ref[0, pl.ds(row_at, tile), :]
                    biases = [jnp.where(kp <= qpos, 0.0, NEGATIVE) for kp in kpos]
                    for spot in range(per_kv // chain):
                        attend(spot, row_at, keys, [page_v[e] for e in range(2)], biases, False)
                    return unused

                lax.fori_loop(tile_from, tiles, one_tile, 0)

        return unused

    lax.fori_loop(0, nch, page, 0)

    if last:
        live = lax.broadcasted_iota(jnp.int32, (rows, HD), 0) < select + lens_here
        for h in range(per_kv):
            result = acc_ref[h, :, :HD] / acc_ref[h, :, HD:]
            out_ref[0, :, h * HD : (h + 1) * HD] = jnp.where(live, result, 0.0).astype(jnp.bfloat16)
    else:
        lane = lax.broadcasted_iota(jnp.int32, m_ref.shape, 2)
        acc_out[0] = acc_ref[:, :, :HD]
        ml_out[0] = jnp.where(lane < HD // 2, m_ref[...], acc_ref[:, :, HD:])


def body(groups_of, fresh_query, fresh_keys, fresh_values, store_keys, store_values, span_ids, span_slot, select_pos, ask_len):
    stores = lax.axis_size("store")
    store_index = lax.axis_index("store")
    core = lax.axis_index("sub")
    req_dev, rows, q_columns = fresh_query.shape
    ch_dev, half, unused = store_keys.shape
    nch = span_ids.shape[1]
    select = select_pos.shape[1]
    span = 2 * half
    context = nch * span
    references = req_dev * nch
    capacity = (references + stores - 1) // stores
    q_heads = q_columns // HD
    kv_used = max(q_heads // GROUP, 1)
    per_kv = q_heads // kv_used
    tile = row_tile(rows)

    piece = jax.ShapeDtypeStruct((capacity, 2, half, kv_used * HD), jnp.bfloat16)
    smem = pl.BlockSpec(memory_space=pltpu.SMEM)
    anywhere = pl.BlockSpec(memory_space=pl.ANY)
    packed = pl.pallas_call(
        functools.partial(pack_kernel, stores, capacity, req_dev, nch, ch_dev, q_heads, kv_used),
        out_shape=[piece] * (2 * stores),
        in_specs=[smem, smem, anywhere, anywhere],
        out_specs=[anywhere] * (2 * stores),
        scratch_shapes=[pltpu.SemaphoreType.DMA((stores * capacity * 4,))],
        name="pack_spans",
    )(span_ids, span_slot, store_keys, store_values)

    pieces = {}
    for group in groups_of(stores):
        for d in group:
            for e in range(2):
                block = packed[2 * d + e]
                if (d, e) != (0, 0):
                    pairs = [
                        (s * 2 + c, ((s + d) % stores) * 2 + (c + e) % 2) for s in range(stores) for c in range(2)
                    ]
                    block = lax.ppermute(block, ("store", "sub"), pairs)
                pieces[(d, e)] = block

    my_pos = lax.dynamic_slice_in_dim(select_pos, store_index * req_dev, req_dev, 0)
    my_len = lax.dynamic_slice_in_dim(ask_len, store_index * req_dev, req_dev, 0)
    my_ids = lax.dynamic_slice_in_dim(span_ids, store_index * req_dev, req_dev, 0).reshape(references)
    my_owners = span_slot[my_ids] // ch_dev
    earlier = jnp.arange(references)[None, :] < jnp.arange(references)[:, None]
    my_ranks = jnp.sum((my_owners[:, None] == my_owners[None, :]) & earlier, axis=1, dtype=jnp.int32)
    my_offsets = (store_index - my_owners + stores) % stores
    chunk_at = jnp.arange(nch, dtype=jnp.int32) * span
    before = jnp.sum(my_pos[:, None, :] < chunk_at[None, :, None], axis=2, dtype=jnp.int32).reshape(references)
    table = jnp.stack([my_offsets, my_ranks, before // tile], axis=1).astype(jnp.int32).reshape(references * 3)
    places = jnp.arange(context, dtype=jnp.int32)
    chosen = jnp.any(my_pos[:, :, None] == places[None, None, :], axis=1)
    key_pos = jnp.where(chosen, FAR, places[None, :]).reshape(req_dev, nch * 2, 1, half)
    tail = jnp.broadcast_to(context + jnp.arange(rows - select, dtype=jnp.int32), (req_dev, rows - select))
    query_pos = jnp.concatenate([my_pos, tail], axis=1)[:, :, None]
    column = (core * q_heads // GROUP).astype(jnp.int32).reshape(1)

    state_block = pl.BlockSpec((1, per_kv, rows, HD), lambda r, n, *s: (r * kv_used + n, 0, 0, 0))
    state_shape = jax.ShapeDtypeStruct((req_dev * kv_used, per_kv, rows, HD), jnp.float32)
    head_block = pl.BlockSpec((1, rows, per_kv * HD), lambda r, n, *s: (r, 0, n))
    fresh_block = pl.BlockSpec((1, rows, HD), lambda r, n, t, l, c: (r, 0, c[0] + n))
    state = []
    steps = groups_of(stores)
    padded = round_up(rows, HD)
    for at, group in enumerate(steps):
        first, last = at == 0, at == len(steps) - 1
        blocks = [pieces[(d, e)] for d in group for e in range(2)]
        in_specs = [
            head_block,
            fresh_block,
            fresh_block,
            pl.BlockSpec((1, rows, 1), lambda r, n, *s: (r, 0, 0)),
            pl.BlockSpec((1, nch * 2, 1, half), lambda r, n, *s: (r, 0, 0, 0)),
        ]
        in_specs += [pl.BlockSpec((capacity, 2, half, HD), lambda r, n, *s: (0, 0, 0, n))] * len(blocks)
        in_specs += [state_block] * len(state)
        flops = 4 * req_dev * q_heads * rows * HD * (context * len(group) // stores // 2 + (rows // 2 if first else 0))
        state = pl.pallas_call(
            functools.partial(
                attend_kernel, tuple(group), first, last, per_kv, nch, select, rows, tile, half
            ),
            grid_spec=pltpu.PrefetchScalarGridSpec(
                num_scalar_prefetch=3,
                grid=(req_dev, kv_used),
                in_specs=in_specs,
                out_specs=[head_block] if last else [state_block] * 2,
                scratch_shapes=[
                    pltpu.VMEM((per_kv, rows, 2 * HD), jnp.float32),
                    pltpu.VMEM((per_kv, rows, HD), jnp.float32),
                    pltpu.VMEM((padded, HD), jnp.bfloat16),
                    pltpu.VMEM((padded, 2 * HD), jnp.bfloat16),
                    pltpu.VMEM((2, half, 2 * HD), jnp.bfloat16),
                ],
            ),
            out_shape=[jax.ShapeDtypeStruct(fresh_query.shape, jnp.bfloat16)] if last else [state_shape] * 2,
            compiler_params=pltpu.CompilerParams(vmem_limit_bytes=VMEM_BYTES),
            cost_estimate=pl.CostEstimate(flops=flops, bytes_accessed=30 << 20, transcendentals=flops // (4 * HD)),
            name="attend_pages",
        )(table, my_len, column, fresh_query, fresh_keys, fresh_values, query_pos, key_pos, *blocks, *state)
    return state[0]


def groups_of(stores):
    near = [d for d in range(1, stores) if min(d, stores - d) <= stores // 4]
    far = [d for d in range(1, stores) if d not in near]
    return [group for group in ([0], near, far) if group]


def solution(mesh):
    placed = (
        P(("groups", "store"), None, ("head", "sub")),
        P(("groups", "store"), None, "head"),
        P(("groups", "store"), None, "head"),
        P(("groups", "store"), "sub", "head"),
        P(("groups", "store"), "sub", "head"),
        P("groups", None),
        P("groups"),
        P("groups", None),
        P("groups"),
    )
    return jax.shard_map(
        functools.partial(body, groups_of),
        mesh=mesh,
        in_specs=placed,
        out_specs=P(("groups", "store"), None, ("head", "sub")),
        check_vma=False,
    )
```

```python
import functools
import math

import jax
import jax.numpy as jnp
from jax import lax
from jax.experimental import pallas as pl
from jax.experimental.pallas import tpu as pltpu
from jax.sharding import PartitionSpec as P

HD = 128
GROUP = 8
NEGATIVE = -1e30
FAR = 1 << 20
CHAIN = 2
VMEM_BYTES = 52 * 1024 * 1024


def row_tile(rows):
    for size in range(192, 15, -16):
        if rows % size == 0:
            return size
    return rows


def round_up(value, unit):
    return (value + unit - 1) // unit * unit


def pack_kernel(stores, plan, req_dev, nch, ch_dev, q_heads, kv_used, ids, slots, keys, values, *outs):
    me = lax.axis_index("store")
    core = lax.axis_index("sub")
    width = kv_used * HD

    for d in sorted({d for d, low, count in plan}):
        target = lax.rem(me + d, stores)

        def visit(j, rank):
            request = target * req_dev + lax.div(j, nch)
            slot = slots[ids[request, lax.rem(j, nch)]]
            place = lax.rem(slot, ch_dev)
            hit = lax.div(slot, ch_dev) == me
            for at, (offset, low, count) in enumerate(plan):
                if offset != d:
                    continue

                @pl.when(hit & (rank >= low) & (rank < low + count))
                def _():
                    for e in range(2):
                        column = pl.multiple_of(lax.rem(core + e, 2) * q_heads // GROUP * HD, HD)
                        for which, source in enumerate((keys, values)):
                            outs[2 * at + e][rank - low, which] = source[place, :, pl.ds(column, width)]

            return rank + hit.astype(jnp.int32)

        lax.fori_loop(0, req_dev * nch, visit, jnp.int32(0))


def attend_kernel(group, first, last, per_kv, nch, select, rows, tile, half, *refs):
    table, lens, column, q_ref, kf_ref, vf_ref, qpos_ref, kpos_ref = refs[:8]
    pieces = refs[8 : 8 + 2 * len(group)]
    rest = list(refs[8 + 2 * len(group) :])
    if not first:
        acc_in, ml_in = rest[:2]
        rest = rest[2:]
    if last:
        out_ref = rest[0]
        rest = rest[1:]
    else:
        acc_out, ml_out = rest[:2]
        rest = rest[2:]
    acc_ref, m_ref, k_scr, v_scr, page_v = rest
    request = pl.program_id(0)
    scale = HD ** (-0.5) * math.log2(math.e)
    chain = min(CHAIN, per_kv)
    tiles = rows // tile
    lens_here = lens[request]

    def wide(value, width):
        return jnp.concatenate([value] * (width // HD), axis=1)

    def score(spot, row_at, keys, biases):
        span = pl.ds(row_at, tile)
        q = jnp.concatenate(
            [q_ref[0, span, (spot * chain + h) * HD : (spot * chain + h + 1) * HD] for h in range(chain)], axis=0
        )
        scores = []
        for k, bias in zip(keys, biases):
            s = lax.dot_general(q, k, (((1,), (1,)), ((), ())), preferred_element_type=jnp.float32)
            s = s.reshape(chain, tile, s.shape[1]) + bias[None]
            scores.append(s.reshape(chain * tile, s.shape[2]))
        return scores

    def weigh(spot, row_at, scores, values, begin):
        heads = pl.ds(spot * chain, chain)
        span = pl.ds(row_at, tile)
        peak = jnp.max(scores[0], axis=-1, keepdims=True)
        for s in scores[1:]:
            peak = jnp.maximum(peak, jnp.max(s, axis=-1, keepdims=True))
        if begin:
            m_new = jnp.broadcast_to(peak, (chain * tile, HD))
        else:
            m_old = m_ref[heads, span, :].reshape(chain * tile, HD)
            m_new = jnp.maximum(m_old, peak)
        update = None
        for s, v in zip(scores, values):
            p = jnp.exp2((s - wide(m_new, s.shape[1])) * scale).astype(jnp.bfloat16)
            part = jnp.dot(p, v, preferred_element_type=jnp.float32)
            update = part if update is None else update + part
        if not begin:
            factor = jnp.exp2((m_old - m_new) * scale)
            update = acc_ref[heads, span, :].reshape(chain * tile, 2 * HD) * wide(factor, 2 * HD) + update
        acc_ref[heads, span, :] = update.reshape(chain, tile, 2 * HD)
        m_ref[heads, span, :] = m_new.reshape(chain, tile, HD)

    def attend(row_at, keys, values, biases, begin):
        spots = per_kv // chain
        ahead = score(0, row_at, keys, biases)
        for spot in range(spots):
            scores = ahead
            if spot + 1 < spots:
                ahead = score(spot + 1, row_at, keys, biases)
            weigh(spot, row_at, scores, values, begin)

    page_v[:, :, HD:] = jnp.ones((2, half, HD), jnp.bfloat16)
    if first:
        padded = k_scr.shape[0]
        k_scr[...] = jnp.zeros(k_scr.shape, jnp.bfloat16)
        v_scr[:, :HD] = jnp.zeros((padded, HD), jnp.bfloat16)
        v_scr[:, HD:] = jnp.ones((padded, HD), jnp.bfloat16)
        k_scr[:rows, :] = kf_ref[0]
        v_scr[:rows, :HD] = vf_ref[0]
        for t in range(tiles):
            end = min(round_up((t + 1) * tile, HD), padded)
            row_id = lax.broadcasted_iota(jnp.int32, (tile, end), 0) + t * tile
            key_id = lax.broadcasted_iota(jnp.int32, (tile, end), 1)
            allowed = (key_id <= row_id) & (key_id < select + lens_here)
            bias = jnp.where(allowed, 0.0, NEGATIVE)
            attend(t * tile, [k_scr[:end, :]], [v_scr[:end, :]], [bias], True)
    else:
        ml = ml_in[0]
        acc_ref[:, :, :HD] = acc_in[0]
        m_ref[...] = jnp.broadcast_to(ml[:, :, :1], ml.shape)
        acc_ref[:, :, HD:] = jnp.broadcast_to(ml[:, :, HD // 2 : HD // 2 + 1], ml.shape)

    core = lax.axis_index("sub")

    def page(chunk, unused):
        base = (request * nch + chunk) * 3
        offset, rank, tile_from = table[base], table[base + 1], table[base + 2]
        for at, (d, low, count) in enumerate(group):

            @pl.when((offset == d) & (rank >= low) & (rank < low + count))
            def _():
                keys = [pieces[2 * at + e][rank - low, 0] for e in range(2)]
                for e in range(2):
                    page_v[e, :, :HD] = pieces[2 * at + e][rank - low, 1]
                kpos = [kpos_ref[0, chunk * 2 + lax.rem(core + e, 2)] for e in range(2)]

                def one_tile(t, unused):
                    row_at = pl.multiple_of(t * tile, 16)
                    qpos = qpos_ref[0, pl.ds(row_at, tile), :]
                    biases = [jnp.where(kp <= qpos, 0.0, NEGATIVE) for kp in kpos]
                    attend(row_at, keys, [page_v[e] for e in range(2)], biases, False)
                    return unused

                lax.fori_loop(tile_from, tiles, one_tile, 0)

        return unused

    lax.fori_loop(0, nch, page, 0)

    if last:
        live = lax.broadcasted_iota(jnp.int32, (rows, HD), 0) < select + lens_here
        for h in range(per_kv):
            result = acc_ref[h, :, :HD] / acc_ref[h, :, HD:]
            out_ref[0, :, h * HD : (h + 1) * HD] = jnp.where(live, result, 0.0).astype(jnp.bfloat16)
    else:
        lane = lax.broadcasted_iota(jnp.int32, m_ref.shape, 2)
        acc_out[0] = acc_ref[:, :, :HD]
        ml_out[0] = jnp.where(lane < HD // 2, m_ref[...], acc_ref[:, :, HD:])


def body(fresh_query, fresh_keys, fresh_values, store_keys, store_values, span_ids, span_slot, select_pos, ask_len):
    stores = lax.axis_size("store")
    store_index = lax.axis_index("store")
    core = lax.axis_index("sub")
    req_dev, rows, q_columns = fresh_query.shape
    ch_dev, half, unused = store_keys.shape
    nch = span_ids.shape[1]
    select = select_pos.shape[1]
    span = 2 * half
    context = nch * span
    references = req_dev * nch
    capacity = (references + stores - 1) // stores
    q_heads = q_columns // HD
    kv_used = max(q_heads // GROUP, 1)
    per_kv = q_heads // kv_used
    tile = row_tile(rows)

    steps = phases(stores, capacity)
    plan = [part for group in steps for part in group]
    smem = pl.BlockSpec(memory_space=pltpu.SMEM)
    vmem = pl.BlockSpec(memory_space=pltpu.VMEM)
    packed = pl.pallas_call(
        functools.partial(pack_kernel, stores, plan, req_dev, nch, ch_dev, q_heads, kv_used),
        out_shape=[
            jax.ShapeDtypeStruct((count, 2, half, kv_used * HD), jnp.bfloat16)
            for d, low, count in plan
            for e in range(2)
        ],
        in_specs=[smem, smem, vmem, vmem],
        out_specs=[vmem] * (2 * len(plan)),
        compiler_params=pltpu.CompilerParams(vmem_limit_bytes=VMEM_BYTES),
        name="pack_spans",
    )(span_ids, span_slot, store_keys, store_values)

    pieces = {}
    for at, part in enumerate(plan):
        for e in range(2):
            d = part[0]
            block = packed[2 * at + e]
            if (d, e) != (0, 0):
                pairs = [(s * 2 + c, ((s + d) % stores) * 2 + (c + e) % 2) for s in range(stores) for c in range(2)]
                block = lax.ppermute(block, ("store", "sub"), pairs)
            pieces[(part, e)] = block

    my_pos = lax.dynamic_slice_in_dim(select_pos, store_index * req_dev, req_dev, 0)
    my_len = lax.dynamic_slice_in_dim(ask_len, store_index * req_dev, req_dev, 0)
    my_ids = lax.dynamic_slice_in_dim(span_ids, store_index * req_dev, req_dev, 0).reshape(references)
    my_owners = span_slot[my_ids] // ch_dev
    earlier = jnp.arange(references)[None, :] < jnp.arange(references)[:, None]
    my_ranks = jnp.sum((my_owners[:, None] == my_owners[None, :]) & earlier, axis=1, dtype=jnp.int32)
    my_offsets = (store_index - my_owners + stores) % stores
    chunk_at = jnp.arange(nch, dtype=jnp.int32) * span
    before = jnp.sum(my_pos[:, None, :] < chunk_at[None, :, None], axis=2, dtype=jnp.int32).reshape(references)
    table = jnp.stack([my_offsets, my_ranks, before // tile], axis=1).astype(jnp.int32).reshape(references * 3)
    places = jnp.arange(context, dtype=jnp.int32)
    chosen = jnp.any(my_pos[:, :, None] == places[None, None, :], axis=1)
    key_pos = jnp.where(chosen, FAR, places[None, :]).reshape(req_dev, nch * 2, 1, half)
    tail = jnp.broadcast_to(context + jnp.arange(rows - select, dtype=jnp.int32), (req_dev, rows - select))
    query_pos = jnp.concatenate([my_pos, tail], axis=1)[:, :, None]
    column = (core * q_heads // GROUP).astype(jnp.int32).reshape(1)

    state_block = pl.BlockSpec((1, per_kv, rows, HD), lambda r, n, *s: (r * kv_used + n, 0, 0, 0))
    state_shape = jax.ShapeDtypeStruct((req_dev * kv_used, per_kv, rows, HD), jnp.float32)
    head_block = pl.BlockSpec((1, rows, per_kv * HD), lambda r, n, *s: (r, 0, n))
    fresh_block = pl.BlockSpec((1, rows, HD), lambda r, n, t, l, c: (r, 0, c[0] + n))
    state = []
    padded = round_up(rows, HD)
    for at, group in enumerate(steps):
        first, last = at == 0, at == len(steps) - 1
        blocks = [pieces[(part, e)] for part in group for e in range(2)]
        spans_here = sum(count for d, low, count in group)
        in_specs = [
            head_block,
            fresh_block,
            fresh_block,
            pl.BlockSpec((1, rows, 1), lambda r, n, *s: (r, 0, 0)),
            pl.BlockSpec((1, nch * 2, 1, half), lambda r, n, *s: (r, 0, 0, 0)),
        ]
        in_specs += [pl.BlockSpec((block.shape[0], 2, half, HD), lambda r, n, *s: (0, 0, 0, n)) for block in blocks]
        in_specs += [state_block] * len(state)
        flops = 4 * req_dev * q_heads * rows * HD * (span * spans_here // req_dev // 2 + (rows // 2 if first else 0))
        state = pl.pallas_call(
            functools.partial(
                attend_kernel, group, first, last, per_kv, nch, select, rows, tile, half
            ),
            grid_spec=pltpu.PrefetchScalarGridSpec(
                num_scalar_prefetch=3,
                grid=(req_dev, kv_used),
                in_specs=in_specs,
                out_specs=[head_block] if last else [state_block] * 2,
                scratch_shapes=[
                    pltpu.VMEM((per_kv, rows, 2 * HD), jnp.float32),
                    pltpu.VMEM((per_kv, rows, HD), jnp.float32),
                    pltpu.VMEM((padded, HD), jnp.bfloat16),
                    pltpu.VMEM((padded, 2 * HD), jnp.bfloat16),
                    pltpu.VMEM((2, half, 2 * HD), jnp.bfloat16),
                ],
            ),
            out_shape=[jax.ShapeDtypeStruct(fresh_query.shape, jnp.bfloat16)] if last else [state_shape] * 2,
            compiler_params=pltpu.CompilerParams(vmem_limit_bytes=VMEM_BYTES),
            cost_estimate=pl.CostEstimate(flops=flops, bytes_accessed=30 << 20, transcendentals=flops // (4 * HD)),
            name="attend_pages",
        )(table, my_len, column, fresh_query, fresh_keys, fresh_values, query_pos, key_pos, *blocks, *state)
    return state[0]


def phases(stores, capacity):
    every = [(d, rank) for d in range(1, stores) for rank in range(capacity)]
    every.sort(key=lambda at: (min(at[0], stores - at[0]), at[1], at[0]))
    total = len(every)
    last = max(total // 9, 1)
    cuts = [0, (total - 3 * last) // 2, total - 3 * last, total - last, total]
    steps = [[(0, 0, capacity)]]
    for begin, end in zip(cuts[:-1], cuts[1:]):
        group = {}
        for d, rank in every[begin:end]:
            group.setdefault(d, []).append(rank)
        if group:
            steps.append([(d, min(ranks), len(ranks)) for d, ranks in group.items()])
    return steps


def solution(mesh):
    placed = (
        P(("groups", "store"), None, ("head", "sub")),
        P(("groups", "store"), None, "head"),
        P(("groups", "store"), None, "head"),
        P(("groups", "store"), "sub", "head"),
        P(("groups", "store"), "sub", "head"),
        P("groups", None),
        P("groups"),
        P("groups", None),
        P("groups"),
    )
    return jax.shard_map(
        body,
        mesh=mesh,
        in_specs=placed,
        out_specs=P(("groups", "store"), None, ("head", "sub")),
        check_vma=False,
    )
```

```python
import functools
import math

import jax
import jax.numpy as jnp
from jax import lax
from jax.experimental import pallas as pl
from jax.experimental.pallas import tpu as pltpu
from jax.sharding import PartitionSpec as P

HD = 128
GROUP = 8
NEGATIVE = -1e30
FAR = 1 << 20
CHAIN = 2
VMEM_BYTES = 52 * 1024 * 1024


def row_tile(rows):
    for size in range(192, 15, -16):
        if rows % size == 0:
            return size
    return rows


def round_up(value, unit):
    return (value + unit - 1) // unit * unit


def pack_kernel(stores, plan, req_dev, nch, ch_dev, q_heads, kv_used, ids, slots, keys, values, *outs):
    me = lax.axis_index("store")
    core = lax.axis_index("sub")
    width = kv_used * HD

    for d in sorted({d for d, low, count in plan}):
        target = lax.rem(me + d, stores)

        def visit(j, rank):
            request = target * req_dev + lax.div(j, nch)
            slot = slots[ids[request, lax.rem(j, nch)]]
            place = lax.rem(slot, ch_dev)
            hit = lax.div(slot, ch_dev) == me
            for at, (offset, low, count) in enumerate(plan):
                if offset != d:
                    continue

                @pl.when(hit & (rank >= low) & (rank < low + count))
                def _():
                    for e in range(2):
                        column = pl.multiple_of(lax.rem(core + e, 2) * q_heads // GROUP * HD, HD)
                        for which, source in enumerate((keys, values)):
                            outs[2 * at + e][rank - low, which] = source[place, :, pl.ds(column, width)]

            return rank + hit.astype(jnp.int32)

        lax.fori_loop(0, req_dev * nch, visit, jnp.int32(0))


def attend_kernel(group, first, last, per_kv, nch, select, rows, tile, half, *refs):
    table, lens, column, q_ref, kf_ref, vf_ref, qpos_ref, kpos_ref = refs[:8]
    pieces = refs[8 : 8 + 2 * len(group)]
    rest = list(refs[8 + 2 * len(group) :])
    if not first:
        acc_in, ml_in = rest[:2]
        rest = rest[2:]
    if last:
        out_ref = rest[0]
        rest = rest[1:]
    else:
        acc_out, ml_out = rest[:2]
        rest = rest[2:]
    acc_ref, m_ref, k_scr, v_scr, page_v = rest
    request = pl.program_id(0)
    scale = HD ** (-0.5) * math.log2(math.e)
    chain = min(CHAIN, per_kv)
    tiles = rows // tile
    lens_here = lens[request]

    def wide(value, width):
        return jnp.concatenate([value] * (width // HD), axis=1)

    def score(spot, row_at, keys, biases):
        span = pl.ds(row_at, tile)
        q = jnp.concatenate(
            [q_ref[0, span, (spot * chain + h) * HD : (spot * chain + h + 1) * HD] for h in range(chain)], axis=0
        )
        scores = []
        for k, bias in zip(keys, biases):
            s = lax.dot_general(q, k, (((1,), (1,)), ((), ())), preferred_element_type=jnp.float32)
            s = s.reshape(chain, tile, s.shape[1]) + bias[None]
            scores.append(s.reshape(chain * tile, s.shape[2]))
        return scores

    def weigh(spot, row_at, scores, values, begin):
        heads = pl.ds(spot * chain, chain)
        span = pl.ds(row_at, tile)
        peak = jnp.max(scores[0], axis=-1, keepdims=True)
        for s in scores[1:]:
            peak = jnp.maximum(peak, jnp.max(s, axis=-1, keepdims=True))
        if begin:
            m_new = jnp.broadcast_to(peak, (chain * tile, HD))
        else:
            m_old = m_ref[heads, span, :].reshape(chain * tile, HD)
            m_new = jnp.maximum(m_old, peak)
        update = None
        for s, v in zip(scores, values):
            p = jnp.exp2((s - wide(m_new, s.shape[1])) * scale).astype(jnp.bfloat16)
            part = jnp.dot(p, v, preferred_element_type=jnp.float32)
            update = part if update is None else update + part
        if not begin:
            factor = jnp.exp2((m_old - m_new) * scale)
            update = acc_ref[heads, span, :].reshape(chain * tile, 2 * HD) * wide(factor, 2 * HD) + update
        acc_ref[heads, span, :] = update.reshape(chain, tile, 2 * HD)
        m_ref[heads, span, :] = m_new.reshape(chain, tile, HD)

    def attend(row_at, keys, values, biases, begin):
        spots = per_kv // chain
        ahead = score(0, row_at, keys, biases)
        for spot in range(spots):
            scores = ahead
            if spot + 1 < spots:
                ahead = score(spot + 1, row_at, keys, biases)
            weigh(spot, row_at, scores, values, begin)

    page_v[:, :, HD:] = jnp.ones((2, half, HD), jnp.bfloat16)
    if first:
        padded = k_scr.shape[0]
        k_scr[...] = jnp.zeros(k_scr.shape, jnp.bfloat16)
        v_scr[:, :HD] = jnp.zeros((padded, HD), jnp.bfloat16)
        v_scr[:, HD:] = jnp.ones((padded, HD), jnp.bfloat16)
        k_scr[:rows, :] = kf_ref[0]
        v_scr[:rows, :HD] = vf_ref[0]
        for t in range(tiles):
            end = min(round_up((t + 1) * tile, HD), padded)
            row_id = lax.broadcasted_iota(jnp.int32, (tile, end), 0) + t * tile
            key_id = lax.broadcasted_iota(jnp.int32, (tile, end), 1)
            allowed = (key_id <= row_id) & (key_id < select + lens_here)
            bias = jnp.where(allowed, 0.0, NEGATIVE)
            attend(t * tile, [k_scr[:end, :]], [v_scr[:end, :]], [bias], True)
    else:
        acc_ref[:, :, :HD] = acc_in[0]
        ml = ml_in[0]
        for h in range(per_kv):
            m_ref[h] = jnp.broadcast_to(ml[:, h : h + 1], (rows, HD))
            acc_ref[h, :, HD:] = jnp.broadcast_to(ml[:, HD // 2 + h : HD // 2 + h + 1], (rows, HD))

    core = lax.axis_index("sub")

    def page(chunk, unused):
        base = (request * nch + chunk) * 3
        offset, rank, tile_from = table[base], table[base + 1], table[base + 2]
        for at, (d, low, count) in enumerate(group):

            @pl.when((offset == d) & (rank >= low) & (rank < low + count))
            def _():
                keys = [pieces[2 * at + e][rank - low, 0] for e in range(2)]
                for e in range(2):
                    page_v[e, :, :HD] = pieces[2 * at + e][rank - low, 1]
                kpos = [kpos_ref[0, chunk * 2 + lax.rem(core + e, 2)] for e in range(2)]

                def one_tile(t, unused):
                    row_at = pl.multiple_of(t * tile, 16)
                    qpos = qpos_ref[0, pl.ds(row_at, tile), :]
                    biases = [jnp.where(kp <= qpos, 0.0, NEGATIVE) for kp in kpos]
                    attend(row_at, keys, [page_v[e] for e in range(2)], biases, False)
                    return unused

                lax.fori_loop(tile_from, tiles, one_tile, 0)

        return unused

    lax.fori_loop(0, nch, page, 0)

    if last:
        live = lax.broadcasted_iota(jnp.int32, (rows, HD), 0) < select + lens_here
        for h in range(per_kv):
            total = acc_ref[h, :, HD:]
            inverse = pl.reciprocal(total, approx=True)
            inverse = inverse * (2.0 - total * inverse)
            result = acc_ref[h, :, :HD] * inverse
            out_ref[0, :, h * HD : (h + 1) * HD] = jnp.where(live, result, 0.0).astype(jnp.bfloat16)
    else:
        acc_out[0] = acc_ref[:, :, :HD]
        lane = lax.broadcasted_iota(jnp.int32, (rows, HD), 1)
        ml = jnp.zeros((rows, HD), jnp.float32)
        for h in range(per_kv):
            ml = jnp.where(lane == h, m_ref[h], ml)
            ml = jnp.where(lane == HD // 2 + h, acc_ref[h, :, HD:], ml)
        ml_out[0] = ml


def body(fresh_query, fresh_keys, fresh_values, store_keys, store_values, span_ids, span_slot, select_pos, ask_len):
    stores = lax.axis_size("store")
    store_index = lax.axis_index("store")
    core = lax.axis_index("sub")
    req_dev, rows, q_columns = fresh_query.shape
    ch_dev, half, unused = store_keys.shape
    nch = span_ids.shape[1]
    select = select_pos.shape[1]
    span = 2 * half
    context = nch * span
    references = req_dev * nch
    capacity = (references + stores - 1) // stores
    q_heads = q_columns // HD
    kv_used = max(q_heads // GROUP, 1)
    per_kv = q_heads // kv_used
    tile = row_tile(rows)

    steps = phases(stores, capacity)
    plan = [part for group in steps for part in group]
    smem = pl.BlockSpec(memory_space=pltpu.SMEM)
    vmem = pl.BlockSpec(memory_space=pltpu.VMEM)
    packed = pl.pallas_call(
        functools.partial(pack_kernel, stores, plan, req_dev, nch, ch_dev, q_heads, kv_used),
        out_shape=[
            jax.ShapeDtypeStruct((count, 2, half, kv_used * HD), jnp.bfloat16)
            for d, low, count in plan
            for e in range(2)
        ],
        in_specs=[smem, smem, vmem, vmem],
        out_specs=[vmem] * (2 * len(plan)),
        compiler_params=pltpu.CompilerParams(vmem_limit_bytes=VMEM_BYTES),
        name="pack_spans",
    )(span_ids, span_slot, store_keys, store_values)

    pieces = {}

    def send(step, gates):
        for part in steps[step]:
            at, d = plan.index(part), part[0]
            for e in range(2):
                block = packed[2 * at + e]
                if (d, e) != (0, 0):
                    if gates:
                        block = lax.optimization_barrier((block, *gates))[0]
                    pairs = [
                        (s * 2 + c, ((s + d) % stores) * 2 + (c + e) % 2) for s in range(stores) for c in range(2)
                    ]
                    block = lax.ppermute(block, ("store", "sub"), pairs)
                pieces[(part, e)] = block

    for step in range(min(3, len(steps))):
        send(step, [])

    my_pos = lax.dynamic_slice_in_dim(select_pos, store_index * req_dev, req_dev, 0)
    my_len = lax.dynamic_slice_in_dim(ask_len, store_index * req_dev, req_dev, 0)
    my_ids = lax.dynamic_slice_in_dim(span_ids, store_index * req_dev, req_dev, 0).reshape(references)
    my_owners = span_slot[my_ids] // ch_dev
    earlier = jnp.arange(references)[None, :] < jnp.arange(references)[:, None]
    my_ranks = jnp.sum((my_owners[:, None] == my_owners[None, :]) & earlier, axis=1, dtype=jnp.int32)
    my_offsets = (store_index - my_owners + stores) % stores
    chunk_at = jnp.arange(nch, dtype=jnp.int32) * span
    before = jnp.sum(my_pos[:, None, :] < chunk_at[None, :, None], axis=2, dtype=jnp.int32).reshape(references)
    table = jnp.stack([my_offsets, my_ranks, before // tile], axis=1).astype(jnp.int32).reshape(references * 3)
    places = jnp.arange(context, dtype=jnp.int32)
    chosen = jnp.any(my_pos[:, :, None] == places[None, None, :], axis=1)
    key_pos = jnp.where(chosen, FAR, places[None, :]).reshape(req_dev, nch * 2, 1, half)
    tail = jnp.broadcast_to(context + jnp.arange(rows - select, dtype=jnp.int32), (req_dev, rows - select))
    query_pos = jnp.concatenate([my_pos, tail], axis=1)[:, :, None]
    column = (core * q_heads // GROUP).astype(jnp.int32).reshape(1)

    state_block = pl.BlockSpec((1, per_kv, rows, HD), lambda r, n, *s: (r * kv_used + n, 0, 0, 0))
    ml_block = pl.BlockSpec((1, rows, HD), lambda r, n, *s: (r * kv_used + n, 0, 0))
    state_shape = [
        jax.ShapeDtypeStruct((req_dev * kv_used, per_kv, rows, HD), jnp.float32),
        jax.ShapeDtypeStruct((req_dev * kv_used, rows, HD), jnp.float32),
    ]
    head_block = pl.BlockSpec((1, rows, per_kv * HD), lambda r, n, *s: (r, 0, n))
    fresh_block = pl.BlockSpec((1, rows, HD), lambda r, n, t, l, c: (r, 0, c[0] + n))
    state = []
    padded = round_up(rows, HD)
    for at, group in enumerate(steps):
        first, last = at == 0, at == len(steps) - 1
        if at == 2 and len(steps) > 3:
            send(3, [state[1][0, 0, :1]])
        blocks = [pieces[(part, e)] for part in group for e in range(2)]
        spans_here = sum(count for d, low, count in group)
        in_specs = [
            head_block,
            fresh_block,
            fresh_block,
            pl.BlockSpec((1, rows, 1), lambda r, n, *s: (r, 0, 0)),
            pl.BlockSpec((1, nch * 2, 1, half), lambda r, n, *s: (r, 0, 0, 0)),
        ]
        in_specs += [pl.BlockSpec((block.shape[0], 2, half, HD), lambda r, n, *s: (0, 0, 0, n)) for block in blocks]
        in_specs += [state_block, ml_block][: len(state)]
        flops = 4 * req_dev * q_heads * rows * HD * (span * spans_here // req_dev // 2 + (rows // 2 if first else 0))
        state = pl.pallas_call(
            functools.partial(
                attend_kernel, group, first, last, per_kv, nch, select, rows, tile, half
            ),
            grid_spec=pltpu.PrefetchScalarGridSpec(
                num_scalar_prefetch=3,
                grid=(req_dev, kv_used),
                in_specs=in_specs,
                out_specs=[head_block] if last else [state_block, ml_block],
                scratch_shapes=[
                    pltpu.VMEM((per_kv, rows, 2 * HD), jnp.float32),
                    pltpu.VMEM((per_kv, rows, HD), jnp.float32),
                    pltpu.VMEM((padded, HD), jnp.bfloat16),
                    pltpu.VMEM((padded, 2 * HD), jnp.bfloat16),
                    pltpu.VMEM((2, half, 2 * HD), jnp.bfloat16),
                ],
            ),
            out_shape=[jax.ShapeDtypeStruct(fresh_query.shape, jnp.bfloat16)] if last else state_shape,
            compiler_params=pltpu.CompilerParams(vmem_limit_bytes=VMEM_BYTES),
            cost_estimate=pl.CostEstimate(flops=flops, bytes_accessed=30 << 20, transcendentals=flops // (4 * HD)),
            name="attend_pages",
        )(table, my_len, column, fresh_query, fresh_keys, fresh_values, query_pos, key_pos, *blocks, *state)
    return state[0]


def phases(stores, capacity):
    every = [(d, rank) for d in range(1, stores) for rank in range(capacity)]
    every.sort(key=lambda at: (min(at[0], stores - at[0]), at[1], at[0]))
    total = len(every)
    last = max(total // 9, 1)
    cuts = [0, total - 3 * last, total - last, total]
    steps = [[(0, 0, capacity)]]
    for begin, end in zip(cuts[:-1], cuts[1:]):
        group = {}
        for d, rank in every[begin:end]:
            group.setdefault(d, []).append(rank)
        if group:
            steps.append([(d, min(ranks), len(ranks)) for d, ranks in group.items()])
    return steps


def solution(mesh):
    placed = (
        P(("groups", "store"), None, ("head", "sub")),
        P(("groups", "store"), None, "head"),
        P(("groups", "store"), None, "head"),
        P(("groups", "store"), "sub", "head"),
        P(("groups", "store"), "sub", "head"),
        P("groups", None),
        P("groups"),
        P("groups", None),
        P("groups"),
    )
    return jax.shard_map(
        body,
        mesh=mesh,
        in_specs=placed,
        out_specs=P(("groups", "store"), None, ("head", "sub")),
        check_vma=False,
    )
```

```python
import functools
import math

import jax
import jax.numpy as jnp
from jax import lax
from jax.experimental import pallas as pl
from jax.experimental.pallas import tpu as pltpu
from jax.sharding import PartitionSpec as P

HD = 128
GROUP = 8
NEGATIVE = -1e30
FAR = 1 << 20
CHAIN = 2
VMEM_BYTES = 52 * 1024 * 1024


def row_tile(rows):
    for size in range(192, 15, -16):
        if rows % size == 0:
            return size
    return rows


def round_up(value, unit):
    return (value + unit - 1) // unit * unit


def pack_kernel(stores, plan, req_dev, nch, ch_dev, q_heads, kv_used, ids, slots, keys, values, *outs):
    me = lax.axis_index("store")
    core = lax.axis_index("sub")
    width = kv_used * HD
    outs[1][0, 0] = jnp.zeros(outs[1].shape[2:], jnp.bfloat16)

    for d in sorted({d for d, low, count in plan}):
        target = lax.rem(me + d, stores)

        def visit(j, rank):
            request = target * req_dev + lax.div(j, nch)
            slot = slots[ids[request, lax.rem(j, nch)]]
            place = lax.rem(slot, ch_dev)
            hit = lax.div(slot, ch_dev) == me
            for at, (offset, low, count) in enumerate(plan):
                if offset != d:
                    continue

                @pl.when(hit & (rank >= low) & (rank < low + count))
                def _():
                    for e in range(2):
                        column = pl.multiple_of(lax.rem(core + e, 2) * q_heads // GROUP * HD, HD)
                        for which, source in enumerate((keys, values)):
                            outs[2 * at + e][rank - low, which] = source[place, :, pl.ds(column, width)]

            return rank + hit.astype(jnp.int32)

        lax.fori_loop(0, req_dev * nch, visit, jnp.int32(0))


def attend_kernel(group, halves, first, last, per_kv, nch, select, rows, tile, half, *refs):
    table, lens, column, q_ref, kf_ref, vf_ref, qpos_ref, kpos_ref = refs[:8]
    pieces = refs[8 : 8 + len(halves) * len(group)]
    rest = list(refs[8 + len(halves) * len(group) :])
    if not first:
        acc_in, ml_in = rest[:2]
        rest = rest[2:]
    if last:
        out_ref = rest[0]
        rest = rest[1:]
    else:
        acc_out, ml_out = rest[:2]
        rest = rest[2:]
    acc_ref, m_ref, k_scr, v_scr, page_v = rest
    request = pl.program_id(0)
    scale = HD ** (-0.5) * math.log2(math.e)
    chain = min(CHAIN, per_kv)
    tiles = rows // tile
    lens_here = lens[request]

    def wide(value, width):
        return jnp.concatenate([value] * (width // HD), axis=1)

    def score(spot, row_at, keys, biases):
        span = pl.ds(row_at, tile)
        q = jnp.concatenate(
            [q_ref[0, span, (spot * chain + h) * HD : (spot * chain + h + 1) * HD] for h in range(chain)], axis=0
        )
        scores = []
        for k, bias in zip(keys, biases):
            s = lax.dot_general(q, k, (((1,), (1,)), ((), ())), preferred_element_type=jnp.float32)
            s = s.reshape(chain, tile, s.shape[1]) + bias[None]
            scores.append(s.reshape(chain * tile, s.shape[2]))
        return scores

    def weigh(spot, row_at, scores, values, begin):
        heads = pl.ds(spot * chain, chain)
        span = pl.ds(row_at, tile)
        peak = jnp.max(scores[0], axis=-1, keepdims=True)
        for s in scores[1:]:
            peak = jnp.maximum(peak, jnp.max(s, axis=-1, keepdims=True))
        if begin:
            m_new = jnp.broadcast_to(peak, (chain * tile, HD))
        else:
            m_old = m_ref[heads, span, :].reshape(chain * tile, HD)
            m_new = jnp.maximum(m_old, peak)
        update = None
        for s, v in zip(scores, values):
            p = jnp.exp2((s - wide(m_new, s.shape[1])) * scale).astype(jnp.bfloat16)
            part = jnp.dot(p, v, preferred_element_type=jnp.float32)
            update = part if update is None else update + part
        if not begin:
            factor = jnp.exp2((m_old - m_new) * scale)
            update = acc_ref[heads, span, :].reshape(chain * tile, 2 * HD) * wide(factor, 2 * HD) + update
        acc_ref[heads, span, :] = update.reshape(chain, tile, 2 * HD)
        m_ref[heads, span, :] = m_new.reshape(chain, tile, HD)

    def attend(row_at, keys, values, biases, begin):
        spots = per_kv // chain
        ahead = score(0, row_at, keys, biases)
        for spot in range(spots):
            scores = ahead
            if spot + 1 < spots:
                ahead = score(spot + 1, row_at, keys, biases)
            weigh(spot, row_at, scores, values, begin)

    page_v[:, :, HD:] = jnp.ones((2, half, HD), jnp.bfloat16)
    if first:
        padded = k_scr.shape[0]
        k_scr[...] = jnp.zeros(k_scr.shape, jnp.bfloat16)
        v_scr[:, :HD] = jnp.zeros((padded, HD), jnp.bfloat16)
        v_scr[:, HD:] = jnp.ones((padded, HD), jnp.bfloat16)
        k_scr[:rows, :] = kf_ref[0]
        v_scr[:rows, :HD] = vf_ref[0]
        for t in range(tiles):
            end = min(round_up((t + 1) * tile, HD), padded)
            row_id = lax.broadcasted_iota(jnp.int32, (tile, end), 0) + t * tile
            key_id = lax.broadcasted_iota(jnp.int32, (tile, end), 1)
            allowed = (key_id <= row_id) & (key_id < select + lens_here)
            bias = jnp.where(allowed, 0.0, NEGATIVE)
            attend(t * tile, [k_scr[:end, :]], [v_scr[:end, :]], [bias], True)
    else:
        acc_ref[:, :, :HD] = acc_in[0]
        ml = ml_in[0]
        for h in range(per_kv):
            m_ref[h] = jnp.broadcast_to(ml[:, h : h + 1], (rows, HD))
            acc_ref[h, :, HD:] = jnp.broadcast_to(ml[:, HD // 2 + h : HD // 2 + h + 1], (rows, HD))

    core = lax.axis_index("sub")

    def page(chunk, unused):
        base = (request * nch + chunk) * 3
        offset, rank, tile_from = table[base], table[base + 1], table[base + 2]
        for at, (d, low, count) in enumerate(group):

            @pl.when((offset == d) & (rank >= low) & (rank < low + count))
            def _():
                here = pieces[len(halves) * at : len(halves) * (at + 1)]
                keys = [piece[rank - low, 0] for piece in here]
                for e, piece in zip(halves, here):
                    page_v[e, :, :HD] = piece[rank - low, 1]
                kpos = [kpos_ref[0, chunk * 2 + lax.rem(core + e, 2)] for e in halves]

                def one_tile(t, unused):
                    row_at = pl.multiple_of(t * tile, 16)
                    qpos = qpos_ref[0, pl.ds(row_at, tile), :]
                    biases = [jnp.where(kp <= qpos, 0.0, NEGATIVE) for kp in kpos]
                    attend(row_at, keys, [page_v[e] for e in halves], biases, False)
                    return unused

                lax.fori_loop(tile_from, tiles, one_tile, 0)

        return unused

    lax.fori_loop(0, nch, page, 0)

    if last:
        live = lax.broadcasted_iota(jnp.int32, (rows, HD), 0) < select + lens_here
        for h in range(per_kv):
            total = acc_ref[h, :, HD:]
            inverse = pl.reciprocal(total, approx=True)
            inverse = inverse * (2.0 - total * inverse)
            result = acc_ref[h, :, :HD] * inverse
            out_ref[0, :, h * HD : (h + 1) * HD] = jnp.where(live, result, 0.0).astype(jnp.bfloat16)
    else:
        acc_out[0] = acc_ref[:, :, :HD]
        lane = lax.broadcasted_iota(jnp.int32, (rows, HD), 1)
        ml = jnp.zeros((rows, HD), jnp.float32)
        for h in range(per_kv):
            ml = jnp.where(lane == h, m_ref[h], ml)
            ml = jnp.where(lane == HD // 2 + h, acc_ref[h, :, HD:], ml)
        ml_out[0] = ml


def body(fresh_query, fresh_keys, fresh_values, store_keys, store_values, span_ids, span_slot, select_pos, ask_len):
    stores = lax.axis_size("store")
    store_index = lax.axis_index("store")
    core = lax.axis_index("sub")
    req_dev, rows, q_columns = fresh_query.shape
    ch_dev, half, unused = store_keys.shape
    nch = span_ids.shape[1]
    select = select_pos.shape[1]
    span = 2 * half
    context = nch * span
    references = req_dev * nch
    capacity = (references + stores - 1) // stores
    q_heads = q_columns // HD
    kv_used = max(q_heads // GROUP, 1)
    per_kv = q_heads // kv_used
    tile = row_tile(rows)

    steps = phases(stores, capacity)
    plan = [part for group in steps for part in group]
    smem = pl.BlockSpec(memory_space=pltpu.SMEM)
    vmem = pl.BlockSpec(memory_space=pltpu.VMEM)
    packed = pl.pallas_call(
        functools.partial(pack_kernel, stores, plan, req_dev, nch, ch_dev, q_heads, kv_used),
        out_shape=[
            jax.ShapeDtypeStruct((count, 2, half, kv_used * HD), jnp.bfloat16)
            for d, low, count in plan
            for e in range(2)
        ],
        in_specs=[smem, smem, vmem, vmem],
        out_specs=[vmem] * (2 * len(plan)),
        compiler_params=pltpu.CompilerParams(vmem_limit_bytes=VMEM_BYTES),
        name="pack_spans",
    )(span_ids, span_slot, store_keys, store_values)

    pieces = {}

    def send(step, e, gates):
        for part in steps[step]:
            at, d = plan.index(part), part[0]
            block = packed[2 * at + e]
            if (d, e) != (0, 0):
                if gates:
                    block = jnp.where(gates[0] == gates[0], block, jnp.zeros_like(block))
                pairs = [(s * 2 + c, ((s + d) % stores) * 2 + (c + e) % 2) for s in range(stores) for c in range(2)]
                block = lax.ppermute(block, ("store", "sub"), pairs)
            pieces[(part, e)] = block

    calls = []
    for step in range(len(steps)):
        far = step == len(steps) - 1 and step > 1
        calls += [(steps[step], (0,)), (steps[step], (1,))] if far else [(steps[step], (0, 1))]
        send(step, 0, [pieces[(plan[0], 1)][0, 0, 0, 0]] if far else [])
        if not far:
            send(step, 1, [])

    my_pos = lax.dynamic_slice_in_dim(select_pos, store_index * req_dev, req_dev, 0)
    my_len = lax.dynamic_slice_in_dim(ask_len, store_index * req_dev, req_dev, 0)
    my_ids = lax.dynamic_slice_in_dim(span_ids, store_index * req_dev, req_dev, 0).reshape(references)
    my_owners = span_slot[my_ids] // ch_dev
    earlier = jnp.arange(references)[None, :] < jnp.arange(references)[:, None]
    my_ranks = jnp.sum((my_owners[:, None] == my_owners[None, :]) & earlier, axis=1, dtype=jnp.int32)
    my_offsets = (store_index - my_owners + stores) % stores
    chunk_at = jnp.arange(nch, dtype=jnp.int32) * span
    before = jnp.sum(my_pos[:, None, :] < chunk_at[None, :, None], axis=2, dtype=jnp.int32).reshape(references)
    table = jnp.stack([my_offsets, my_ranks, before // tile], axis=1).astype(jnp.int32).reshape(references * 3)
    places = jnp.arange(context, dtype=jnp.int32)
    chosen = jnp.any(my_pos[:, :, None] == places[None, None, :], axis=1)
    key_pos = jnp.where(chosen, FAR, places[None, :]).reshape(req_dev, nch * 2, 1, half)
    tail = jnp.broadcast_to(context + jnp.arange(rows - select, dtype=jnp.int32), (req_dev, rows - select))
    query_pos = jnp.concatenate([my_pos, tail], axis=1)[:, :, None]
    column = (core * q_heads // GROUP).astype(jnp.int32).reshape(1)

    state_block = pl.BlockSpec((1, per_kv, rows, HD), lambda r, n, *s: (r * kv_used + n, 0, 0, 0))
    ml_block = pl.BlockSpec((1, rows, HD), lambda r, n, *s: (r * kv_used + n, 0, 0))
    state_shape = [
        jax.ShapeDtypeStruct((req_dev * kv_used, per_kv, rows, HD), jnp.float32),
        jax.ShapeDtypeStruct((req_dev * kv_used, rows, HD), jnp.float32),
    ]
    head_block = pl.BlockSpec((1, rows, per_kv * HD), lambda r, n, *s: (r, 0, n))
    fresh_block = pl.BlockSpec((1, rows, HD), lambda r, n, t, l, c: (r, 0, c[0] + n))
    state = []
    padded = round_up(rows, HD)
    for at, (group, halves) in enumerate(calls):
        first, last = at == 0, at == len(calls) - 1
        if at == 1 and len(calls) > 3:
            send(2, 1, [state[1][0, 0, 0]])
        blocks = [pieces[(part, e)] for part in group for e in halves]
        spans_here = sum(count for d, low, count in group)
        in_specs = [
            head_block,
            fresh_block,
            fresh_block,
            pl.BlockSpec((1, rows, 1), lambda r, n, *s: (r, 0, 0)),
            pl.BlockSpec((1, nch * 2, 1, half), lambda r, n, *s: (r, 0, 0, 0)),
        ]
        in_specs += [pl.BlockSpec((block.shape[0], 2, half, HD), lambda r, n, *s: (0, 0, 0, n)) for block in blocks]
        in_specs += [state_block, ml_block][: len(state)]
        flops = 4 * req_dev * q_heads * rows * HD * (half * len(halves) * spans_here // req_dev // 2 + (rows // 2 if first else 0))
        state = pl.pallas_call(
            functools.partial(
                attend_kernel, group, halves, first, last, per_kv, nch, select, rows, tile, half
            ),
            grid_spec=pltpu.PrefetchScalarGridSpec(
                num_scalar_prefetch=3,
                grid=(req_dev, kv_used),
                in_specs=in_specs,
                out_specs=[head_block] if last else [state_block, ml_block],
                scratch_shapes=[
                    pltpu.VMEM((per_kv, rows, 2 * HD), jnp.float32),
                    pltpu.VMEM((per_kv, rows, HD), jnp.float32),
                    pltpu.VMEM((padded, HD), jnp.bfloat16),
                    pltpu.VMEM((padded, 2 * HD), jnp.bfloat16),
                    pltpu.VMEM((2, half, 2 * HD), jnp.bfloat16),
                ],
            ),
            out_shape=[jax.ShapeDtypeStruct(fresh_query.shape, jnp.bfloat16)] if last else state_shape,
            compiler_params=pltpu.CompilerParams(vmem_limit_bytes=VMEM_BYTES),
            cost_estimate=pl.CostEstimate(flops=flops, bytes_accessed=30 << 20, transcendentals=flops // (4 * HD)),
            name="attend_pages",
        )(table, my_len, column, fresh_query, fresh_keys, fresh_values, query_pos, key_pos, *blocks, *state)
    return state[0]


def phases(stores, capacity):
    every = [(d, rank) for d in range(1, stores) for rank in range(capacity)]
    every.sort(key=lambda at: (min(at[0], stores - at[0]), at[1], at[0]))
    total = len(every)
    cuts = [0, total - total // 3, total]
    steps = [[(0, 0, capacity)]]
    for begin, end in zip(cuts[:-1], cuts[1:]):
        group = {}
        for d, rank in every[begin:end]:
            group.setdefault(d, []).append(rank)
        if group:
            steps.append([(d, min(ranks), len(ranks)) for d, ranks in group.items()])
    return steps


def solution(mesh):
    placed = (
        P(("groups", "store"), None, ("head", "sub")),
        P(("groups", "store"), None, "head"),
        P(("groups", "store"), None, "head"),
        P(("groups", "store"), "sub", "head"),
        P(("groups", "store"), "sub", "head"),
        P("groups", None),
        P("groups"),
        P("groups", None),
        P("groups"),
    )
    return jax.shard_map(
        body,
        mesh=mesh,
        in_specs=placed,
        out_specs=P(("groups", "store"), None, ("head", "sub")),
        check_vma=False,
    )
```
